256 devices in a mesh: gx: 16 (over x_lo, z), gy: 8 (over y, core), gz: 2 (over x_hi).
Axes of the slice: x: 4 (x_hi: 2, x_lo: 2; x = x_hi * 2 + x_lo), y: 4, z: 8, core: 2. Of those that a mesh axis runs over, the one named last changes fastest.
Arguments:
- integrals: bfloat16 [1024, 8, 100, 1024], P('gx', None, 'gz', 'gy'), may hold values from -6 to 6
- amplitude: bfloat16 [100, 1024, 1024], P('gz', 'gx', 'gy'), may hold values from -0.0546875 to 0.0546875
- virtual_irrep: int32 [32], replicated, may hold values from 0 to 7, as said below
- occupied_irrep: int32 [6], replicated, may hold values from 0 to 7
Outputs:
- cycle_term: float32 [1024, 8, 1024], P('gx', None, ('gy', 'gz'))
The draws below stay inside these ranges and needn't reach their ends.
Inputs may be any that keep to these rules, and one draw needn't show every extreme that they name: `virtual_irrep`: every one of the 8 irreps labels at least one block of virtual orbitals. `occupied_irrep`: the first 4 entries label the blocks of 25 occupied orbitals k, the next one the i block, the last one the j orbital.
All inputs are finite; a program needn't handle non-finite values.
Results may differ from the reference program's by a relative error of at most 0.0003.
Values may be sent and summed in bfloat16 or wider, within the bound.
No kernel may reach another device: no remote copies, remote signals or barrier semaphores. Data moves between devices by JAX's collectives and lax.ppermute only.
A program may use at most 64 MiB of HBM per device.

```python
import jax
import jax.numpy as jnp
from jax import lax

V = 1024
K = 100
VB = 32
KB = 25
OI = 8


def draw_virtual_irrep(key, part):
    key = jax.random.fold_in(key, 5)
    first, second = jax.random.split(key)
    labels = jax.random.randint(first, (V // VB,), 0, 8)
    spots = jax.random.permutation(second, V // VB)[:8]
    return labels.at[spots].set(jnp.arange(8, dtype=jnp.int32)).astype(jnp.int32)


def place_ends(values, rng, least, high):
    longest = values.shape.index(max(values.shape))
    spots = []
    for shift in (0, 1):
        where = [jax.random.randint(jax.random.fold_in(rng, axis), (), 0, length) for axis, length in enumerate(values.shape)]
        where[longest] = (where[longest] + shift) % values.shape[longest]
        spots.append(tuple(where))
    return values.at[spots[0]].set(least).at[spots[1]].set(high)


def block_scale(key, extent, shards, low, top_value):
    loudness = 1.0
    for dim, blocks in shards:
        steps = jax.random.uniform(jax.random.fold_in(jax.random.fold_in(key, 6), dim), (blocks,), jnp.float32, low / len(shards), top_value / len(shards))
        loudness = loudness * jnp.repeat(jnp.exp(steps), extent[dim] // blocks).reshape((-1,) + (1,) * (len(extent) - 1 - dim))
    return loudness


def scatter_about(stream_key, dims, deviation, limit, pieces=(), kind=jnp.bfloat16):
    array = deviation * jax.random.normal(stream_key, dims, jnp.float32)
    if pieces:
        array = array * block_scale(stream_key, dims, pieces, -0.22, 0.18)
    return jnp.clip(array, -limit, limit).astype(kind)


def setup_inputs(seed: int = 0) -> dict:
    keys = jax.random.split(jax.random.key(seed), 5)
    integrals = scatter_about(keys[0], (V, OI, K, V), 1.0, 6.0, ((0, 16), (2, 2), (3, 8)))
    amplitude = scatter_about(keys[1], (K, V, V), (K * V // 8) ** -0.5, 0.0546875, ((0, 2), (1, 16), (2, 8)))
    virtual_irrep = draw_virtual_irrep(jax.random.fold_in(keys[4], 71), 0)
    occupied_irrep = place_ends(jax.random.randint(keys[3], (K // KB + 2,), 0, 8), jax.random.fold_in(keys[3], 1), 0, 7).astype(jnp.int32)
    return {"integrals": integrals, "amplitude": amplitude, "virtual_irrep": virtual_irrep, "occupied_irrep": occupied_irrep}


def reference(integrals, amplitude, virtual_irrep, occupied_irrep):
    vlabels = jnp.repeat(virtual_irrep, VB)
    klabels = jnp.repeat(occupied_irrep[: K // KB], KB)
    irrep_left = occupied_irrep[K // KB]
    irrep_right = occupied_irrep[K // KB + 1]
    pair_virtual = jnp.bitwise_xor(vlabels[:, None], vlabels[None, :])

    def step(total, index):
        slab = lax.dynamic_index_in_dim(integrals, index, 2, keepdims=False)
        block = lax.dynamic_index_in_dim(amplitude, index, 0, keepdims=False)
        k_label = klabels[index]
        keep_left = jnp.bitwise_xor(pair_virtual, jnp.bitwise_xor(irrep_left, k_label)) == 0
        keep_right = jnp.bitwise_xor(pair_virtual, jnp.bitwise_xor(irrep_right, k_label)) == 0
        left = jnp.where(keep_left[:, None, :], slab, jnp.zeros((), slab.dtype))
        right = jnp.where(keep_right, block, jnp.zeros((), block.dtype))
        product = lax.dot_general(left.reshape(V * OI, V), right, (((1,), (1,)), ((), ())), preferred_element_type=jnp.float32)
        return total + product.reshape(V, OI, V), None

    start = jnp.zeros((V, OI, V), jnp.float32)
    total, unused = lax.scan(step, start, jnp.arange(K, dtype=jnp.int32))
    return total
```

```python
import functools

import jax
import jax.numpy as jnp
from jax import lax
from jax.experimental import pallas as pl
from jax.experimental.pallas import tpu as pltpu
from jax.sharding import PartitionSpec as P

K = 100
VB = 32
KB = 25
HALF = 13
SLOTS = 8
SMEM = pltpu.MemorySpace.SMEM
VMEM = pltpu.MemorySpace.VMEM
I32 = jnp.int32
F32 = jnp.float32
BF16 = jnp.bfloat16


def tier_kernel(lv, lo, out):
    rows = lax.broadcasted_iota(I32, (32, 128), 0)
    lanes = lax.broadcasted_iota(I32, (32, 128), 1)
    col = jnp.zeros((32, 128), I32)
    row = jnp.full((32, 128), 64, I32)
    for block in range(32):
        col = jnp.where(rows == block, lv[block], col)
        row = jnp.where(lanes == block, lv[block], row)
    left, right = lo[4], lo[5]
    both = jnp.bitwise_xor(col, row)
    even = (jnp.bitwise_and(rows, 1) == 0) & (lanes < 32)
    load = jnp.zeros((), I32)
    for part in range(2):
        total = jnp.zeros((32, 128), I32)
        for kap in range(2):
            total += jnp.where(both == jnp.bitwise_xor(lo[2 * part + kap], right), 1, 0)
        total = total + pltpu.roll(total, 127, 1)
        total = total + pltpu.roll(total, 126, 1)
        total = total + pltpu.roll(total, 31, 0)
        load = jnp.maximum(load, jnp.max(jnp.where(even & (jnp.bitwise_and(lanes, 3) == 0), total, 0)))
    most = jnp.max(jnp.sum(jnp.where(both == 0, 1, 0), axis=1))
    twin = (col == pltpu.roll(col, 31, 0)) & (row == pltpu.roll(row, 127, 1))
    full = even & (jnp.bitwise_and(lanes, 1) == 0) & twin & (both == jnp.bitwise_xor(left, right))
    four = jnp.max(jnp.where(full, 1, 0))
    step = jnp.where(load <= 4, 0, jnp.where(load <= 6, 1, 2))
    fits = (load <= 8) & (most <= SLOTS)
    out[0] = jnp.where(fits, 2 * step + four, 6)


def pack_kernel(groups, lv, lo, amp, out):
    gy, gz = lax.axis_index("gy"), lax.axis_index("gz")
    gx = lax.axis_index("gx")
    lanes = lax.broadcasted_iota(I32, (HALF, 32, 128), 2)
    out[...] = jnp.zeros_like(out)

    def step(index, unit):
        beta, kap, gam = index // 8, (index // 4) % 2, index % 4
        key = lo[2 * gz + kap] ^ lv[4 * gy + gam] ^ lv[2 * gx + beta] ^ lo[5]

        @pl.when(key == 0)
        def _():
            spot = jnp.bitwise_and(unit, 1) * 64
            group = unit // 2
            value = out[group].astype(F32)
            for half in range(2):
                part = amp[pl.ds(kap * KB + 12 * half, HALF), pl.ds(pl.multiple_of(beta * 32, 32), 32), :]
                to = spot + 32 * half
                moved = pltpu.roll(part.astype(F32), jnp.bitwise_and(to - gam * 32 + 128, 127), 2)
                value = jnp.where((lanes >= to) & (lanes < to + 32), moved, value)
            out[group] = value.astype(BF16)

        return unit + jnp.where(key == 0, 1, 0)

    lax.fori_loop(0, 16, step, jnp.zeros((), I32))


def main_kernel(groups, width, lv, lo, w_hbm, *refs):
    chunks = refs[:16]
    keep, send = refs[16:18]
    w, got, t, acc, pairs, units, blocks, counts, w_sem, sems = refs[18:]
    gx, gy, gz = lax.axis_index("gx"), lax.axis_index("gy"), lax.axis_index("gz")
    x, z = gx // 8, gx % 8
    load_w = pltpu.make_async_copy(w_hbm, w, w_sem)
    load_w.start()
    loads = [pltpu.make_async_copy(chunks[i], got.at[i], sems.at[i]) for i in range(16)]
    for load in loads:
        load.start()
    t[...] = jnp.zeros_like(t)
    keep[...] = jnp.zeros_like(keep)
    send[...] = jnp.zeros_like(send)

    shift = lo[4] ^ lo[5]
    labels = [lv[2 * gx + alpha] ^ shift for alpha in range(2)]
    for label in range(8):
        units[label] = 0
    counts[0] = 0
    counts[1] = 0
    for kap in range(2):
        for gam in range(4):
            label = lo[2 * gz + kap] ^ lv[4 * gy + gam] ^ lo[5]
            for alpha in range(2):
                @pl.when(label == labels[alpha])
                def _():
                    pairs[alpha, units[label]] = kap * 4 + gam
            units[label] = units[label] + 1
    kept = [units[labels[alpha]] for alpha in range(2)]
    lanes = lax.broadcasted_iota(I32, (HALF, 32, 128), 2)
    for load in loads:
        load.wait()

    def arrival(step, _):
        p, beta = step // 2, step % 2
        source = (x ^ (p // 8)) * 8 + ((z + p) % 8)
        block = 2 * source + beta
        label = lv[block]
        first = jnp.where(beta == 0, 0, units[lv[2 * source]])
        for alpha in range(2):
            @pl.when(label == labels[alpha])
            def _():
                slot = counts[alpha]
                blocks[alpha, slot] = block
                counts[alpha] = slot + 1

                def place(r, _):
                    unit = first + r
                    pair = pairs[alpha, r]
                    kap, gam = pair // 4, pair % 4
                    spot = jnp.bitwise_and(unit, 1) * 64
                    whole = got[p, unit // 2].astype(F32)
                    for half in range(2):
                        moved = pltpu.roll(whole, jnp.bitwise_and(gam * 32 - spot - 32 * half + 256, 127), 2)
                        at = (alpha, pl.ds(kap * KB + 12 * half, HALF), pl.ds(pl.multiple_of(slot * 32, 32), 32), slice(None))
                        old = t[at].astype(F32)
                        inside = (lanes >= gam * 32) & (lanes < gam * 32 + 32)
                        t[at] = jnp.where(inside, moved, old).astype(BF16)
                    return 0

                lax.fori_loop(0, kept[alpha], place, 0)
        return 0

    lax.fori_loop(0, 32, arrival, 0)
    load_w.wait()

    for alpha in range(2):
        acc[alpha] = jnp.zeros((32 * SLOTS, 256), F32)

        def multiply(step, _):
            lhs, rhs = [], []
            for i in range(10):
                k = step * 10 + i
                lhs.append(t[alpha, k])
                rhs.append(w[alpha * 32 : alpha * 32 + 32, k].reshape(256, 128))
            acc[alpha] += lax.dot_general(
                jnp.concatenate(lhs, axis=1),
                jnp.concatenate(rhs, axis=1),
                (((1,), (1,)), ((), ())),
                preferred_element_type=F32,
            )
            return 0

        lax.fori_loop(0, 5, multiply, 0)

    core = gy % 2
    for alpha in range(2):
        def give(j, _):
            block = blocks[alpha, j]
            dest, beta = block // 2, block % 2
            if width == 4:
                rank = alpha * 2 + beta
            else:
                rank = jnp.where((beta == 1) & (lv[2 * dest] == labels[alpha]), 1, 0)
                if alpha == 1:
                    for other in range(2):
                        rank = rank + jnp.where(lv[2 * dest + other] == labels[0], 1, 0)
            place = (dest // 4) * 2 + dest % 2
            value = acc[alpha, pl.ds(pl.multiple_of(j * 32, 32), 32), :]
            mine = (dest // 2) % 2 == core

            @pl.when(mine)
            def _():
                keep[place, rank] = value

            @pl.when(jnp.logical_not(mine))
            def _():
                send[place, rank] = value

            return 0

        lax.fori_loop(0, counts[alpha], give, 0)


def last_kernel(width, lv, lo, parts, out):
    gx, gy, gz = lax.axis_index("gx"), lax.axis_index("gy"), lax.axis_index("gz")
    dest = gy * 2 + gz
    shift = lo[4] ^ lo[5]
    count = jnp.zeros((), I32)
    for alpha in range(2):
        label = lv[2 * gx + alpha] ^ shift
        cols = []
        for beta in range(2):
            hit = lv[2 * dest + beta] == label
            rank = alpha * 2 + beta if width == 4 else jnp.minimum(count, 1)
            total = parts[0, rank]
            for i in range(1, 8):
                total = total + parts[i, rank]
            cols.append(jnp.where(hit, total, 0.0))
            count = count + jnp.where(hit, 1, 0)
        out[alpha * 256 : alpha * 256 + 256, :] = jnp.concatenate(cols, axis=0).T


def gather_ring(mine):
    up = [(i, (i // 8) * 8 + (i + 1) % 8) for i in range(16)]
    down = [(i, (i // 8) * 8 + (i + 7) % 8) for i in range(16)]
    cross = [(i, (i + 8) % 16) for i in range(16)]
    zp = lambda v: lax.ppermute(v, "gx", up)
    zm = lambda v: lax.ppermute(v, "gx", down)
    xx = lambda v: lax.ppermute(v, "gx", cross)
    p1, m1, o0 = zp(mine), zm(mine), xx(mine)
    p2, m2, o1 = zp(p1), zm(m1), xx(m1)
    p3, m3, o7 = zp(p2), zm(m2), xx(p1)
    p4, o2, o3 = zp(p3), zm(o1), xx(m3)
    o6, o4, o5 = zp(o7), zm(o3), xx(p3)
    return [mine, m1, m2, m3, p4, p3, p2, p1, o0, o1, o2, o3, o4, o5, o6, o7]


def sparse(groups, width, integrals, amplitude, virtual_irrep, occupied_irrep):
    smem = pl.BlockSpec(memory_space=SMEM)
    vmem = pl.BlockSpec(memory_space=VMEM)
    hbm = pl.BlockSpec(memory_space=pl.ANY)
    chunk = (groups, HALF, 32, 128)
    params = pltpu.CompilerParams(vmem_limit_bytes=48 * 2**20)
    packed = pl.pallas_call(
        functools.partial(pack_kernel, groups),
        out_shape=jax.ShapeDtypeStruct(chunk, BF16),
        in_specs=[smem, smem, vmem],
        out_specs=vmem,
        compiler_params=params,
        name="pack",
    )(virtual_irrep, occupied_irrep, amplitude)
    chunks = gather_ring(packed)
    keep, send = pl.pallas_call(
        functools.partial(main_kernel, groups, width),
        out_shape=[jax.ShapeDtypeStruct((8, width, 32, 256), F32)] * 2,
        in_specs=[smem, smem, hbm] + [hbm] * 16,
        out_specs=[vmem, vmem],
        scratch_shapes=[
            pltpu.VMEM((64, 50, 8, 128), BF16),
            pltpu.VMEM((16,) + chunk, BF16),
            pltpu.VMEM((2, 50, 32 * SLOTS, 128), BF16),
            pltpu.VMEM((2, 32 * SLOTS, 256), F32),
            pltpu.SMEM((2, 8), I32),
            pltpu.SMEM((8,), I32),
            pltpu.SMEM((2, 32), I32),
            pltpu.SMEM((2,), I32),
            pltpu.SemaphoreType.DMA,
            pltpu.SemaphoreType.DMA((16,)),
        ],
        compiler_params=params,
        name="main",
    )(virtual_irrep, occupied_irrep, jnp.transpose(integrals, (0, 2, 1, 3)), *chunks)
    other = lax.ppermute(send, "gy", [(i, i ^ 1) for i in range(8)])
    same_core = [[y * 4 + core * 2 + g for y in range(4) for g in range(2)] for core in range(2)]
    parts = lax.all_to_all(keep + other, ("gy", "gz"), 0, 0, tiled=True, axis_index_groups=same_core)
    out = pl.pallas_call(
        functools.partial(last_kernel, width),
        out_shape=jax.ShapeDtypeStruct((512, 64), F32),
        in_specs=[smem, smem, vmem],
        out_specs=vmem,
        compiler_params=params,
        name="last",
    )(virtual_irrep, occupied_irrep, parts)
    return out.reshape(64, 8, 64)


def dense(integrals, amplitude, virtual_irrep, occupied_irrep):
    rows_a, width_i, rows_k, rows_c = integrals.shape
    vlabels = jnp.repeat(virtual_irrep, VB)
    klabels = jnp.repeat(occupied_irrep[: K // KB], KB)
    irrep_left = occupied_irrep[K // KB]
    irrep_right = occupied_irrep[K // KB + 1]
    a_labels = lax.dynamic_slice_in_dim(vlabels, lax.axis_index("gx") * rows_a, rows_a)
    c_labels = lax.dynamic_slice_in_dim(vlabels, lax.axis_index("gy") * rows_c, rows_c)
    k_labels = lax.dynamic_slice_in_dim(klabels, lax.axis_index("gz") * rows_k, rows_k)
    left_key = a_labels[:, None, None] ^ k_labels[None, :, None] ^ c_labels[None, None, :] ^ irrep_left
    masked = jnp.where((left_key == 0)[:, None, :, :], integrals, jnp.zeros((), integrals.dtype))
    masked = masked.reshape(rows_a * width_i, rows_k, rows_c)
    right_key = k_labels[:, None] ^ c_labels[None, :] ^ irrep_right
    piece = lax.all_gather(amplitude, "gx", axis=1, tiled=True)
    keep_amp = (right_key[:, None, :] ^ vlabels[None, :, None]) == 0
    terms = lax.dot_general(
        masked,
        jnp.where(keep_amp, piece, jnp.zeros((), piece.dtype)),
        (((1, 2), (0, 2)), ((), ())),
        preferred_element_type=F32,
    )
    share = lax.psum_scatter(terms, ("gy", "gz"), scatter_dimension=1, tiled=True)
    return share.reshape(rows_a, width_i, share.shape[1])


def body(integrals, amplitude, virtual_irrep, occupied_irrep):
    smem = pl.BlockSpec(memory_space=SMEM)
    tier = pl.pallas_call(
        tier_kernel,
        out_shape=jax.ShapeDtypeStruct((1,), I32),
        in_specs=[smem, smem],
        out_specs=smem,
        name="tier",
    )(virtual_irrep, occupied_irrep)
    branches = [functools.partial(sparse, groups, width) for groups in (2, 3, 4) for width in (2, 4)]
    return lax.switch(tier[0], branches + [dense], integrals, amplitude, virtual_irrep, occupied_irrep)


def solution(mesh):
    return jax.shard_map(
        body,
        mesh=mesh,
        in_specs=(P("gx", None, "gz", "gy"), P("gz", "gx", "gy"), P(), P()),
        out_specs=P("gx", None, ("gy", "gz")),
        check_vma=False,
    )
```

```python
import functools

import jax
import jax.numpy as jnp
from jax import lax
from jax.experimental import pallas as pl
from jax.experimental.pallas import tpu as pltpu
from jax.sharding import PartitionSpec as P

K = 100
VB = 32
KB = 25
HALF = 13
SLOTS = 8
SMEM = pltpu.MemorySpace.SMEM
VMEM = pltpu.MemorySpace.VMEM
I32 = jnp.int32
F32 = jnp.float32
BF16 = jnp.bfloat16


def tier_kernel(lv, lo, out):
    rows = lax.broadcasted_iota(I32, (32, 128), 0)
    lanes = lax.broadcasted_iota(I32, (32, 128), 1)
    col = jnp.zeros((32, 128), I32)
    row = jnp.full((32, 128), 64, I32)
    for block in range(32):
        col = jnp.where(rows == block, lv[block], col)
        row = jnp.where(lanes == block, lv[block], row)
    left, right = lo[4], lo[5]
    both = jnp.bitwise_xor(col, row)
    even = (jnp.bitwise_and(rows, 1) == 0) & (lanes < 32)
    load = jnp.zeros((), I32)
    for part in range(2):
        total = jnp.zeros((32, 128), I32)
        for kap in range(2):
            total += jnp.where(both == jnp.bitwise_xor(lo[2 * part + kap], right), 1, 0)
        total = total + pltpu.roll(total, 127, 1)
        total = total + pltpu.roll(total, 126, 1)
        total = total + pltpu.roll(total, 31, 0)
        load = jnp.maximum(load, jnp.max(jnp.where(even & (jnp.bitwise_and(lanes, 3) == 0), total, 0)))
    most = jnp.max(jnp.sum(jnp.where(both == 0, 1, 0), axis=1))
    twin = (col == pltpu.roll(col, 31, 0)) & (row == pltpu.roll(row, 127, 1))
    full = even & (jnp.bitwise_and(lanes, 1) == 0) & twin & (both == jnp.bitwise_xor(left, right))
    four = jnp.max(jnp.where(full, 1, 0))
    step = jnp.where(load <= 4, 0, jnp.where(load <= 6, 1, 2))
    fits = (load <= 8) & (most <= SLOTS)
    out[0] = jnp.where(fits, 2 * step + four, 6)


def pack_kernel(groups, lv, lo, amp, out):
    gy, gz = lax.axis_index("gy"), lax.axis_index("gz")
    gx = lax.axis_index("gx")
    lanes = lax.broadcasted_iota(I32, (HALF, 32, 128), 2)
    out[...] = jnp.zeros_like(out)

    def step(index, unit):
        beta, kap, gam = index // 8, (index // 4) % 2, index % 4
        key = lo[2 * gz + kap] ^ lv[4 * gy + gam] ^ lv[2 * gx + beta] ^ lo[5]

        @pl.when(key == 0)
        def _():
            spot = jnp.bitwise_and(unit, 1) * 64
            group = unit // 2
            value = out[group].astype(F32)
            for half in range(2):
                part = amp[pl.ds(kap * KB + 12 * half, HALF), pl.ds(pl.multiple_of(beta * 32, 32), 32), :]
                to = spot + 32 * half
                moved = pltpu.roll(part.astype(F32), jnp.bitwise_and(to - gam * 32 + 128, 127), 2)
                value = jnp.where((lanes >= to) & (lanes < to + 32), moved, value)
            out[group] = value.astype(BF16)

        return unit + jnp.where(key == 0, 1, 0)

    lax.fori_loop(0, 16, step, jnp.zeros((), I32))


def main_kernel(groups, width, lv, lo, w_hbm, *refs):
    chunks = refs[:16]
    keep, send = refs[16:18]
    w, got, t, acc, pairs, units, blocks, counts, w_sem, sems = refs[18:]
    gx, gy, gz = lax.axis_index("gx"), lax.axis_index("gy"), lax.axis_index("gz")
    x, z = gx // 8, gx % 8
    load_w = pltpu.make_async_copy(w_hbm, w, w_sem)
    load_w.start()
    loads = [pltpu.make_async_copy(chunks[i], got.at[i], sems.at[i]) for i in range(16)]
    for load in loads:
        load.start()
    t[...] = jnp.zeros_like(t)
    keep[...] = jnp.zeros_like(keep)
    send[...] = jnp.zeros_like(send)

    shift = lo[4] ^ lo[5]
    labels = [lv[2 * gx + alpha] ^ shift for alpha in range(2)]
    for label in range(8):
        units[label] = 0
    counts[0] = 0
    counts[1] = 0
    for kap in range(2):
        for gam in range(4):
            label = lo[2 * gz + kap] ^ lv[4 * gy + gam] ^ lo[5]
            for alpha in range(2):
                @pl.when(label == labels[alpha])
                def _():
                    pairs[alpha, units[label]] = kap * 4 + gam
            units[label] = units[label] + 1
    kept = [units[labels[alpha]] for alpha in range(2)]
    lanes = lax.broadcasted_iota(I32, (HALF, 32, 128), 2)
    for load in loads:
        load.wait()

    def arrival(step, _):
        p, beta = step // 2, step % 2
        source = (x ^ (p // 8)) * 8 + ((z + p) % 8)
        block = 2 * source + beta
        label = lv[block]
        first = jnp.where(beta == 0, 0, units[lv[2 * source]])
        for alpha in range(2):
            @pl.when(label == labels[alpha])
            def _():
                slot = counts[alpha]
                blocks[alpha, slot] = block
                counts[alpha] = slot + 1

                def place(r, _):
                    unit = first + r
                    pair = pairs[alpha, r]
                    kap, gam = pair // 4, pair % 4
                    spot = jnp.bitwise_and(unit, 1) * 64
                    whole = got[p, unit // 2].astype(F32)
                    for half in range(2):
                        moved = pltpu.roll(whole, jnp.bitwise_and(gam * 32 - spot - 32 * half + 256, 127), 2)
                        at = (alpha, pl.ds(kap * KB + 12 * half, HALF), pl.ds(pl.multiple_of(slot * 32, 32), 32), slice(None))
                        old = t[at].astype(F32)
                        inside = (lanes >= gam * 32) & (lanes < gam * 32 + 32)
                        t[at] = jnp.where(inside, moved, old).astype(BF16)
                    return 0

                lax.fori_loop(0, kept[alpha], place, 0)
        return 0

    lax.fori_loop(0, 32, arrival, 0)
    load_w.wait()

    for alpha in range(2):
        acc[alpha] = jnp.zeros((32 * SLOTS, 256), F32)

        def multiply(step, _):
            lhs, rhs = [], []
            for i in range(10):
                k = step * 10 + i
                lhs.append(t[alpha, k])
                rhs.append(w[alpha * 32 : alpha * 32 + 32, k].reshape(256, 128))
            acc[alpha] += lax.dot_general(
                jnp.concatenate(lhs, axis=1),
                jnp.concatenate(rhs, axis=1),
                (((1,), (1,)), ((), ())),
                preferred_element_type=F32,
            )
            return 0

        lax.fori_loop(0, 5, multiply, 0)

    core = gy % 2
    for alpha in range(2):
        def give(j, _):
            block = blocks[alpha, j]
            dest, beta = block // 2, block % 2
            if width == 4:
                rank = alpha * 2 + beta
            else:
                rank = jnp.where((beta == 1) & (lv[2 * dest] == labels[alpha]), 1, 0)
                if alpha == 1:
                    for other in range(2):
                        rank = rank + jnp.where(lv[2 * dest + other] == labels[0], 1, 0)
            place = (dest // 4) * 2 + dest % 2
            value = acc[alpha, pl.ds(pl.multiple_of(j * 32, 32), 32), :]
            mine = (dest // 2) % 2 == core

            @pl.when(mine)
            def _():
                keep[place, rank] = value

            @pl.when(jnp.logical_not(mine))
            def _():
                send[place, rank] = value

            return 0

        lax.fori_loop(0, counts[alpha], give, 0)


def last_kernel(width, lv, lo, parts, out):
    gx, gy, gz = lax.axis_index("gx"), lax.axis_index("gy"), lax.axis_index("gz")
    dest = gy * 2 + gz
    shift = lo[4] ^ lo[5]
    count = jnp.zeros((), I32)
    for alpha in range(2):
        label = lv[2 * gx + alpha] ^ shift
        cols = []
        for beta in range(2):
            hit = lv[2 * dest + beta] == label
            rank = alpha * 2 + beta if width == 4 else jnp.minimum(count, 1)
            total = parts[0, rank]
            for i in range(1, 8):
                total = total + parts[i, rank]
            cols.append(jnp.where(hit, total, 0.0))
            count = count + jnp.where(hit, 1, 0)
        out[alpha * 256 : alpha * 256 + 256, :] = jnp.concatenate(cols, axis=0).T


def gather_ring(mine):
    up = [(i, (i // 8) * 8 + (i + 1) % 8) for i in range(16)]
    down = [(i, (i // 8) * 8 + (i + 7) % 8) for i in range(16)]
    cross = [(i, (i + 8) % 16) for i in range(16)]
    zp = lambda v: lax.ppermute(v, "gx", up)
    zm = lambda v: lax.ppermute(v, "gx", down)
    xx = lambda v: lax.ppermute(v, "gx", cross)
    hold = lax.optimization_barrier
    p1, m1, o0 = hold((zp(mine), zm(mine), xx(mine)))
    p2, m2, o1 = hold((zp(p1), zm(m1), xx(m1)))
    p3, m3, o7 = hold((zp(p2), zm(m2), xx(p1)))
    p4, o2, o3 = hold((zp(p3), zm(o1), xx(m3)))
    o6, o4, o5 = hold((zp(o7), zm(o3), xx(p3)))
    return [mine, m1, m2, m3, p4, p3, p2, p1, o0, o1, o2, o3, o4, o5, o6, o7]


def sparse(groups, width, integrals, amplitude, virtual_irrep, occupied_irrep):
    smem = pl.BlockSpec(memory_space=SMEM)
    vmem = pl.BlockSpec(memory_space=VMEM)
    hbm = pl.BlockSpec(memory_space=pl.ANY)
    chunk = (groups, HALF, 32, 128)
    params = pltpu.CompilerParams(vmem_limit_bytes=48 * 2**20)
    packed = pl.pallas_call(
        functools.partial(pack_kernel, groups),
        out_shape=jax.ShapeDtypeStruct(chunk, BF16),
        in_specs=[smem, smem, vmem],
        out_specs=vmem,
        compiler_params=params,
        name="pack",
    )(virtual_irrep, occupied_irrep, amplitude)
    chunks = gather_ring(packed)
    keep, send = pl.pallas_call(
        functools.partial(main_kernel, groups, width),
        out_shape=[jax.ShapeDtypeStruct((8, width, 32, 256), F32)] * 2,
        in_specs=[smem, smem, hbm] + [hbm] * 16,
        out_specs=[vmem, vmem],
        scratch_shapes=[
            pltpu.VMEM((64, 50, 8, 128), BF16),
            pltpu.VMEM((16,) + chunk, BF16),
            pltpu.VMEM((2, 50, 32 * SLOTS, 128), BF16),
            pltpu.VMEM((2, 32 * SLOTS, 256), F32),
            pltpu.SMEM((2, 8), I32),
            pltpu.SMEM((8,), I32),
            pltpu.SMEM((2, 32), I32),
            pltpu.SMEM((2,), I32),
            pltpu.SemaphoreType.DMA,
            pltpu.SemaphoreType.DMA((16,)),
        ],
        compiler_params=params,
        name="main",
    )(virtual_irrep, occupied_irrep, jnp.transpose(integrals, (0, 2, 1, 3)), *chunks)
    other = lax.ppermute(send, "gy", [(i, i ^ 1) for i in range(8)])
    same_core = [[y * 4 + core * 2 + g for y in range(4) for g in range(2)] for core in range(2)]
    parts = lax.all_to_all(keep + other, ("gy", "gz"), 0, 0, tiled=True, axis_index_groups=same_core)
    out = pl.pallas_call(
        functools.partial(last_kernel, width),
        out_shape=jax.ShapeDtypeStruct((512, 64), F32),
        in_specs=[smem, smem, vmem],
        out_specs=vmem,
        compiler_params=params,
        name="last",
    )(virtual_irrep, occupied_irrep, parts)
    return out.reshape(64, 8, 64)


def dense(integrals, amplitude, virtual_irrep, occupied_irrep):
    rows_a, width_i, rows_k, rows_c = integrals.shape
    vlabels = jnp.repeat(virtual_irrep, VB)
    klabels = jnp.repeat(occupied_irrep[: K // KB], KB)
    irrep_left = occupied_irrep[K // KB]
    irrep_right = occupied_irrep[K // KB + 1]
    a_labels = lax.dynamic_slice_in_dim(vlabels, lax.axis_index("gx") * rows_a, rows_a)
    c_labels = lax.dynamic_slice_in_dim(vlabels, lax.axis_index("gy") * rows_c, rows_c)
    k_labels = lax.dynamic_slice_in_dim(klabels, lax.axis_index("gz") * rows_k, rows_k)
    left_key = a_labels[:, None, None] ^ k_labels[None, :, None] ^ c_labels[None, None, :] ^ irrep_left
    masked = jnp.where((left_key == 0)[:, None, :, :], integrals, jnp.zeros((), integrals.dtype))
    masked = masked.reshape(rows_a * width_i, rows_k, rows_c)
    right_key = k_labels[:, None] ^ c_labels[None, :] ^ irrep_right
    around = gather_ring(amplitude)
    x, z = lax.axis_index("gx") // 8, lax.axis_index("gx") % 8
    piece = jnp.stack([jnp.concatenate(around[:8], axis=1), jnp.concatenate(around[8:], axis=1)])
    piece = jnp.roll(piece.reshape(2, rows_k, 8, 64, rows_c), (x, z), (0, 2))
    piece = piece.transpose(1, 0, 2, 3, 4).reshape(rows_k, 1024, rows_c)
    keep_amp = (right_key[:, None, :] ^ vlabels[None, :, None]) == 0
    terms = lax.dot_general(
        masked,
        jnp.where(keep_amp, piece, jnp.zeros((), piece.dtype)),
        (((1, 2), (0, 2)), ((), ())),
        preferred_element_type=F32,
    )
    terms = terms.reshape(rows_a * width_i, 16, 64).transpose(1, 0, 2)
    share = lax.all_to_all(terms, ("gy", "gz"), 0, 0, tiled=True).sum(0)
    return share.reshape(rows_a, width_i, 64)


def body(integrals, amplitude, virtual_irrep, occupied_irrep):
    smem = pl.BlockSpec(memory_space=SMEM)
    tier = pl.pallas_call(
        tier_kernel,
        out_shape=jax.ShapeDtypeStruct((1,), I32),
        in_specs=[smem, smem],
        out_specs=smem,
        name="tier",
    )(virtual_irrep, occupied_irrep)
    args = integrals, amplitude, virtual_irrep, occupied_irrep
    out = sparse(4, 4, *args)
    return lax.cond(tier[0] == 6, lambda: dense(*args), lambda: out)


def solution(mesh):
    return jax.shard_map(
        body,
        mesh=mesh,
        in_specs=(P("gx", None, "gz", "gy"), P("gz", "gx", "gy"), P(), P()),
        out_specs=P("gx", None, ("gy", "gz")),
        check_vma=False,
    )
```

```python
import jax
import jax.numpy as jnp
from jax import lax
from jax.experimental import pallas as pl
from jax.experimental.pallas import tpu as pltpu
from jax.sharding import PartitionSpec as P

K = 100
VB = 32
KB = 25
HALF = 13
GROUPS = 3
SLOTS = 8
SMEM = pltpu.MemorySpace.SMEM
VMEM = pltpu.MemorySpace.VMEM
I32 = jnp.int32
F32 = jnp.float32
BF16 = jnp.bfloat16


def tier_kernel(lv, lo, out):
    rows = lax.broadcasted_iota(I32, (32, 128), 0)
    lanes = lax.broadcasted_iota(I32, (32, 128), 1)
    col = jnp.zeros((32, 128), I32)
    row = jnp.full((32, 128), 64, I32)
    for block in range(32):
        col = jnp.where(rows == block, lv[block], col)
        row = jnp.where(lanes == block, lv[block], row)
    right = lo[5]
    both = jnp.bitwise_xor(col, row)
    even = (jnp.bitwise_and(rows, 1) == 0) & (lanes < 32)
    load = jnp.zeros((), I32)
    for part in range(2):
        total = jnp.zeros((32, 128), I32)
        for kap in range(2):
            total += jnp.where(both == jnp.bitwise_xor(lo[2 * part + kap], right), 1, 0)
        for shift in (127, 126, 124):
            total = total + pltpu.roll(total, shift, 1)
        total = total + pltpu.roll(total, 31, 0)
        load = jnp.maximum(load, jnp.max(jnp.where(even & (jnp.bitwise_and(lanes, 7) == 0), total, 0)))
    most = jnp.max(jnp.sum(jnp.where(both == 0, 1, 0), axis=1))
    out[0] = jnp.where((load <= 4 * GROUPS) & (most <= SLOTS), 0, 1)


def pack_kernel(lv, lo, own, other, out):
    gx, gy, gz = lax.axis_index("gx"), lax.axis_index("gy"), lax.axis_index("gz")
    core = gy % 2
    lanes = lax.broadcasted_iota(I32, (HALF, 32, 128), 2)
    out[...] = jnp.zeros_like(out)
    room = 2 * GROUPS

    def add(amp, plane, mine):
        def step(index, carry):
            seen, unit = carry
            beta, kap, gam = index // 8, (index // 4) % 2, index % 4
            hit = lo[2 * gz + kap] ^ lv[4 * (gy - core + plane) + gam] ^ lv[2 * gx + beta] ^ lo[5] == 0
            put = hit & ((seen < room) == mine)

            @pl.when(put)
            def _():
                spot = (unit % 2) * 64
                value = out[unit // 2].astype(F32)
                for half in range(2):
                    part = amp[pl.ds(kap * KB + 12 * half, HALF), pl.ds(pl.multiple_of(beta * 32, 32), 32), :]
                    to = spot + 32 * half
                    moved = pltpu.roll(part.astype(F32), jnp.bitwise_and(to - gam * 32 + 128, 127), 2)
                    value = jnp.where((lanes >= to) & (lanes < to + 32), moved, value)
                out[unit // 2] = value.astype(BF16)

            return seen + jnp.where(hit, 1, 0), unit + jnp.where(put, 1, 0)

        return lambda unit: lax.fori_loop(0, 16, step, (jnp.zeros((), I32), unit))[1]

    unit = add(own, core, True)(jnp.zeros((), I32))
    add(other, 1 - core, False)(unit)


def main_kernel(lv, lo, w_own, w_other, *refs):
    chunks = refs[:16]
    keep, send = refs[16:18]
    w, spare, t, acc, pairs, units, blocks, busy, w_sem, spare_sem = refs[18:]
    gx, gy, gz = lax.axis_index("gx"), lax.axis_index("gy"), lax.axis_index("gz")
    core = gy % 2
    x, z = gx // 8, gx % 8
    load_w = pltpu.make_async_copy(w_own, w, w_sem)
    load_w.start()
    keep[...] = jnp.zeros_like(keep)
    send[...] = jnp.zeros_like(send)
    room = 2 * GROUPS

    shift = lo[4] ^ lo[5]
    for plane in range(2):
        for label in range(8):
            units[plane, label] = 0
    for plane in range(2):
        first_c = 4 * (gy if plane == 0 else gy + 1 - 2 * core)
        for kap in range(2):
            for gam in range(4):
                label = lo[2 * gz + kap] ^ lv[first_c + gam] ^ lo[5]
                spot = units[plane, label]
                for alpha in range(2):
                    @pl.when(label == lv[2 * gx + alpha] ^ shift)
                    def _():
                        pairs[alpha * 16 + plane * 8 + spot] = kap * 4 + gam
                units[plane, label] = spot + 1
    lanes = lax.broadcasted_iota(I32, (HALF, 32, 128), 2)

    def half_of_a(alpha, _):
        want = lv[2 * gx + alpha] ^ shift
        for block in range(4):
            busy[block] = 0

        slot = jnp.zeros((), I32)
        for p in range(16):
            source = (x ^ (p // 8)) * 8 + ((z + p) % 8)

            def arrival(beta, slot, p=p, source=source):
                block = 2 * source + beta
                hit = lv[block] == want

                @pl.when(hit)
                def _():
                    blocks[slot] = block
                    own_first = jnp.where(beta == 0, 0, units[0, lv[2 * source]])
                    far_first = jnp.where(beta == 0, 0, units[1, lv[2 * source]])
                    own_here = units[0, lv[2 * source]] + units[0, lv[2 * source + 1]]
                    near = jnp.clip(room - own_first, 0, units[0, want])
                    skip = jnp.clip(room - far_first, 0, units[1, want])
                    total = near + units[1, want] - skip

                    def place(i, _):
                        far = jnp.where(i < near, 0, 1)
                        r = jnp.where(far == 0, i, i - near + skip)
                        unit = jnp.where(far == 0, own_first + r, own_here + far_first + r - room)
                        pair = pairs[alpha * 16 + far * 8 + r]
                        line, gam = far * 2 + pair // 4, pair % 4

                        @pl.when(busy[line] == 0)
                        def _():
                            t[pl.ds(line * KB, KB)] = jnp.zeros((KB, 32 * SLOTS, 128), BF16)
                            busy[line] = 1

                        spot = (unit % 2) * 64
                        whole = chunks[p][unit // 2].astype(F32)
                        inside = (lanes >= gam * 32) & (lanes < gam * 32 + 32)
                        for half in range(2):
                            moved = pltpu.roll(whole, jnp.bitwise_and(gam * 32 - spot - 32 * half + 256, 127), 2)
                            at = (pl.ds(line * KB + 12 * half, HALF), pl.ds(pl.multiple_of(slot * 32, 32), 32), slice(None))
                            t[at] = jnp.where(inside, moved, t[at].astype(F32)).astype(BF16)
                        return 0

                    lax.fori_loop(0, total, place, 0)

                return slot + jnp.where(hit, 1, 0)

            slot = lax.fori_loop(0, 2, arrival, slot)

        @pl.when(alpha == 0)
        def _():
            load_w.wait()

        acc[...] = jnp.zeros_like(acc)

        def multiply(block, _):
            def run(source, row, first):
                lhs = [t[block * KB + k] for k in range(KB)]
                rhs = [source[pl.ds(row, 32), first + k].reshape(256, 128) for k in range(KB)]
                acc[...] += lax.dot_general(
                    jnp.concatenate(lhs, axis=1),
                    jnp.concatenate(rhs, axis=1),
                    (((1,), (1,)), ((), ())),
                    preferred_element_type=F32,
                )

            @pl.when(busy[block] == 1)
            def _():
                @pl.when(block >= 2)
                def _():
                    part = w_other.at[pl.ds(alpha * 32, 32), pl.ds((block - 2) * KB, KB)]
                    load = pltpu.make_async_copy(part, spare, spare_sem)
                    load.start()
                    load.wait()
                    run(spare, 0, 0)

                @pl.when(block < 2)
                def _():
                    run(w, alpha * 32, block * KB)

            return 0

        lax.fori_loop(0, 4, multiply, 0)

        def give(j, _):
            value = acc[pl.ds(pl.multiple_of(j * 32, 32), 32), :]

            @pl.when(alpha == core)
            def _():
                keep[blocks[j]] = value

            @pl.when(alpha != core)
            def _():
                send[blocks[j]] = value

            return 0

        lax.fori_loop(0, slot, give, 0)
        return 0

    lax.fori_loop(0, 2, half_of_a, 0)


def last_kernel(lv, lo, parts, out):
    gx, gy, gz = lax.axis_index("gx"), lax.axis_index("gy"), lax.axis_index("gz")
    dest = gy * 2 + gz
    shift = lo[4] ^ lo[5]
    for alpha in range(2):
        label = lv[2 * gx + alpha] ^ shift
        cols = []
        for beta in range(2):
            total = jnp.zeros((32, 256), F32)
            for y in range(4):
                for g in range(2):
                    total = total + parts[2 * (y * 4 + alpha * 2 + g) + beta]
            cols.append(jnp.where(lv[2 * dest + beta] == label, total, 0.0))
        out[alpha * 256 : alpha * 256 + 256, :] = jnp.concatenate(cols, axis=0).T


def gather_ring(mine):
    up = [(i, (i // 8) * 8 + (i + 1) % 8) for i in range(16)]
    down = [(i, (i // 8) * 8 + (i + 7) % 8) for i in range(16)]
    cross = [(i, (i + 8) % 16) for i in range(16)]
    zp = lambda v: lax.ppermute(v, "gx", up)
    zm = lambda v: lax.ppermute(v, "gx", down)
    xx = lambda v: lax.ppermute(v, "gx", cross)
    hold = lax.optimization_barrier
    p1, m1, o0 = hold((zp(mine), zm(mine), xx(mine)))
    p2, m2, o1 = hold((zp(p1), zm(m1), xx(m1)))
    p3, m3, o7 = hold((zp(p2), zm(m2), xx(p1)))
    p4, o2, o3 = hold((zp(p3), zm(o1), xx(m3)))
    o6, o4, o5 = hold((zp(o7), zm(o3), xx(p3)))
    return [mine, m1, m2, m3, p4, p3, p2, p1, o0, o1, o2, o3, o4, o5, o6, o7]


def sparse(tier, integrals, amplitude, virtual_irrep, occupied_irrep):
    smem = pl.BlockSpec(memory_space=SMEM)
    vmem = pl.BlockSpec(memory_space=VMEM)
    hbm = pl.BlockSpec(memory_space=pl.ANY)
    chunk = (GROUPS, HALF, 32, 128)
    params = pltpu.CompilerParams(vmem_limit_bytes=32 * 2**20)
    swap = lambda v: lax.ppermute(v, "gy", [(i, i ^ 1) for i in range(8)])
    w = jnp.transpose(integrals, (0, 2, 1, 3))
    amp_other, tier = lax.optimization_barrier((swap(amplitude), tier))
    packed = pl.pallas_call(
        pack_kernel,
        out_shape=jax.ShapeDtypeStruct(chunk, BF16),
        in_specs=[smem, smem, vmem, vmem],
        out_specs=vmem,
        compiler_params=params,
        name="pack",
    )(virtual_irrep, occupied_irrep, amplitude, amp_other)
    packed, w = lax.optimization_barrier((packed, w))
    w_other = swap(w)
    chunks = gather_ring(packed)
    keep, send = pl.pallas_call(
        main_kernel,
        out_shape=[jax.ShapeDtypeStruct((32, 32, 256), F32)] * 2,
        in_specs=[smem, smem, hbm, hbm] + [vmem] * 16,
        out_specs=[vmem, vmem],
        scratch_shapes=[
            pltpu.VMEM((64, 50, 8, 128), BF16),
            pltpu.VMEM((32, KB, 8, 128), BF16),
            pltpu.VMEM((100, 32 * SLOTS, 128), BF16),
            pltpu.VMEM((32 * SLOTS, 256), F32),
            pltpu.SMEM((32,), I32),
            pltpu.SMEM((2, 8), I32),
            pltpu.SMEM((32,), I32),
            pltpu.SMEM((4,), I32),
            pltpu.SemaphoreType.DMA,
            pltpu.SemaphoreType.DMA,
        ],
        compiler_params=params,
        name="main",
    )(virtual_irrep, occupied_irrep, w, w_other, *chunks)
    parts = lax.all_to_all(keep + swap(send), ("gy", "gz"), 0, 0, tiled=True)
    out = pl.pallas_call(
        last_kernel,
        out_shape=jax.ShapeDtypeStruct((512, 64), F32),
        in_specs=[smem, smem, vmem],
        out_specs=vmem,
        compiler_params=params,
        name="last",
    )(virtual_irrep, occupied_irrep, parts)
    return out.reshape(64, 8, 64), tier


def dense(integrals, amplitude, virtual_irrep, occupied_irrep):
    rows_a, width_i, rows_k, rows_c = integrals.shape
    vlabels = jnp.repeat(virtual_irrep, VB)
    klabels = jnp.repeat(occupied_irrep[: K // KB], KB)
    irrep_left = occupied_irrep[K // KB]
    irrep_right = occupied_irrep[K // KB + 1]
    a_labels = lax.dynamic_slice_in_dim(vlabels, lax.axis_index("gx") * rows_a, rows_a)
    c_labels = lax.dynamic_slice_in_dim(vlabels, lax.axis_index("gy") * rows_c, rows_c)
    k_labels = lax.dynamic_slice_in_dim(klabels, lax.axis_index("gz") * rows_k, rows_k)
    left_key = a_labels[:, None, None] ^ k_labels[None, :, None] ^ c_labels[None, None, :] ^ irrep_left
    masked = jnp.where((left_key == 0)[:, None, :, :], integrals, jnp.zeros((), integrals.dtype))
    masked = masked.reshape(rows_a * width_i, rows_k, rows_c)
    right_key = k_labels[:, None] ^ c_labels[None, :] ^ irrep_right
    around = gather_ring(amplitude)
    x, z = lax.axis_index("gx") // 8, lax.axis_index("gx") % 8
    piece = jnp.stack([jnp.concatenate(around[:8], axis=1), jnp.concatenate(around[8:], axis=1)])
    piece = jnp.roll(piece.reshape(2, rows_k, 8, 64, rows_c), (x, z), (0, 2))
    piece = piece.transpose(1, 0, 2, 3, 4).reshape(rows_k, 1024, rows_c)
    keep_amp = (right_key[:, None, :] ^ vlabels[None, :, None]) == 0
    terms = lax.dot_general(
        masked,
        jnp.where(keep_amp, piece, jnp.zeros((), piece.dtype)),
        (((1, 2), (0, 2)), ((), ())),
        preferred_element_type=F32,
    )
    terms = terms.reshape(rows_a * width_i, 16, 64).transpose(1, 0, 2)
    share = lax.all_to_all(terms, ("gy", "gz"), 0, 0, tiled=True).sum(0)
    return share.reshape(rows_a, width_i, 64)


def body(integrals, amplitude, virtual_irrep, occupied_irrep):
    smem = pl.BlockSpec(memory_space=SMEM)
    tier = pl.pallas_call(
        tier_kernel,
        out_shape=jax.ShapeDtypeStruct((1,), I32),
        in_specs=[smem, smem],
        out_specs=smem,
        name="tier",
    )(virtual_irrep, occupied_irrep)
    args = integrals, amplitude, virtual_irrep, occupied_irrep
    out, tier = sparse(tier, *args)
    return lax.cond(tier[0] == 1, lambda: dense(*args), lambda: out)


def solution(mesh):
    return jax.shard_map(
        body,
        mesh=mesh,
        in_specs=(P("gx", None, "gz", "gy"), P("gz", "gx", "gy"), P(), P()),
        out_specs=P("gx", None, ("gy", "gz")),
        check_vma=False,
    )
```

```python
import jax
import jax.numpy as jnp
from jax import lax
from jax.experimental import pallas as pl
from jax.experimental.pallas import tpu as pltpu
from jax.sharding import PartitionSpec as P

K = 100
VB = 32
KB = 25
HALF = 13
GROUPS = 3
SLOTS = 8
SMEM = pltpu.MemorySpace.SMEM
VMEM = pltpu.MemorySpace.VMEM
I32 = jnp.int32
F32 = jnp.float32
BF16 = jnp.bfloat16


def tier_kernel(lv, lo, out):
    rows = lax.broadcasted_iota(I32, (32, 128), 0)
    lanes = lax.broadcasted_iota(I32, (32, 128), 1)
    col = jnp.zeros((32, 128), I32)
    row = jnp.full((32, 128), 64, I32)
    for block in range(32):
        col = jnp.where(rows == block, lv[block], col)
        row = jnp.where(lanes == block, lv[block], row)
    right = lo[5]
    both = jnp.bitwise_xor(col, row)
    even = (jnp.bitwise_and(rows, 1) == 0) & (lanes < 32)
    load = jnp.zeros((), I32)
    for part in range(2):
        total = jnp.zeros((32, 128), I32)
        for kap in range(2):
            total += jnp.where(both == jnp.bitwise_xor(lo[2 * part + kap], right), 1, 0)
        for shift in (127, 126, 124):
            total = total + pltpu.roll(total, shift, 1)
        total = total + pltpu.roll(total, 31, 0)
        load = jnp.maximum(load, jnp.max(jnp.where(even & (jnp.bitwise_and(lanes, 7) == 0), total, 0)))
    out[0] = jnp.where(load <= 4 * GROUPS, 0, 1)


def pack_kernel(lv, lo, own, other, out):
    gx, gy, gz = lax.axis_index("gx"), lax.axis_index("gy"), lax.axis_index("gz")
    core = gy % 2
    lanes = lax.broadcasted_iota(I32, (HALF, 32, 128), 2)
    out[...] = jnp.zeros_like(out)
    room = 2 * GROUPS

    def add(amp, plane, mine):
        def step(index, carry):
            seen, unit = carry
            beta, kap, gam = index // 8, (index // 4) % 2, index % 4
            hit = lo[2 * gz + kap] ^ lv[4 * (gy - core + plane) + gam] ^ lv[2 * gx + beta] ^ lo[5] == 0
            put = hit & ((seen < room) == mine) & (unit < room)

            @pl.when(put)
            def _():
                spot = (unit % 2) * 64
                value = out[unit // 2].astype(F32)
                for half in range(2):
                    part = amp[pl.ds(kap * KB + 12 * half, HALF), pl.ds(pl.multiple_of(beta * 32, 32), 32), :]
                    to = spot + 32 * half
                    moved = pltpu.roll(part.astype(F32), jnp.bitwise_and(to - gam * 32 + 128, 127), 2)
                    value = jnp.where((lanes >= to) & (lanes < to + 32), moved, value)
                out[unit // 2] = value.astype(BF16)

            return seen + jnp.where(hit, 1, 0), unit + jnp.where(put, 1, 0)

        return lambda unit: lax.fori_loop(0, 16, step, (jnp.zeros((), I32), unit))[1]

    unit = add(own, core, True)(jnp.zeros((), I32))
    add(other, 1 - core, False)(unit)


def main_kernel(lv, lo, w_own, w_other, *refs):
    chunks = refs[:16]
    keep, send = refs[16:18]
    w, spare, t, acc, pairs, units, blocks, busy, w_sem, spare_sem = refs[18:]
    gx, gy, gz = lax.axis_index("gx"), lax.axis_index("gy"), lax.axis_index("gz")
    core = gy % 2
    x, z = gx // 8, gx % 8
    load_w = pltpu.make_async_copy(w_own, w, w_sem)
    load_w.start()
    keep[...] = jnp.zeros_like(keep)
    send[...] = jnp.zeros_like(send)
    room = 2 * GROUPS

    shift = lo[4] ^ lo[5]
    for plane in range(2):
        for label in range(8):
            units[plane, label] = 0
    for plane in range(2):
        first_c = 4 * (gy if plane == 0 else gy + 1 - 2 * core)
        for kap in range(2):
            for gam in range(4):
                label = lo[2 * gz + kap] ^ lv[first_c + gam] ^ lo[5]
                spot = units[plane, label]
                for alpha in range(2):
                    @pl.when(label == lv[2 * gx + alpha] ^ shift)
                    def _():
                        pairs[alpha * 16 + plane * 8 + spot] = kap * 4 + gam
                units[plane, label] = spot + 1
    lanes = lax.broadcasted_iota(I32, (HALF, 32, 128), 2)

    def count_both(i, most):
        return tuple(n + jnp.where(lv[i] == lv[2 * gx + a] ^ shift, 1, 0) for a, n in enumerate(most))

    most = lax.fori_loop(0, 32, count_both, (jnp.zeros((), I32), jnp.zeros((), I32)))
    windows = (jnp.maximum(most[0], most[1]) + SLOTS - 1) // SLOTS

    def half_of_a(index, _):
        alpha, window = index // windows, index % windows
        want = lv[2 * gx + alpha] ^ shift
        for block in range(4):
            busy[block] = 0

        slot = -SLOTS * window
        for p in range(16):
            source = (x ^ (p // 8)) * 8 + ((z + p) % 8)

            def arrival(beta, slot, p=p, source=source):
                block = 2 * source + beta
                hit = lv[block] == want

                @pl.when(hit & (slot >= 0) & (slot < SLOTS))
                def _():
                    blocks[slot] = block
                    own_first = jnp.where(beta == 0, 0, units[0, lv[2 * source]])
                    far_first = jnp.where(beta == 0, 0, units[1, lv[2 * source]])
                    own_here = units[0, lv[2 * source]] + units[0, lv[2 * source + 1]]
                    near = jnp.clip(room - own_first, 0, units[0, want])
                    skip = jnp.clip(room - far_first, 0, units[1, want])
                    total = near + units[1, want] - skip

                    def place(i, _):
                        far = jnp.where(i < near, 0, 1)
                        r = jnp.where(far == 0, i, i - near + skip)
                        unit = jnp.minimum(jnp.where(far == 0, own_first + r, own_here + far_first + r - room), room - 1)
                        pair = pairs[alpha * 16 + far * 8 + r]
                        line, gam = far * 2 + pair // 4, pair % 4

                        @pl.when(busy[line] == 0)
                        def _():
                            t[pl.ds(line * KB, KB)] = jnp.zeros((KB, 32 * SLOTS, 128), BF16)
                            busy[line] = 1

                        spot = (unit % 2) * 64
                        whole = chunks[p][unit // 2].astype(F32)
                        inside = (lanes >= gam * 32) & (lanes < gam * 32 + 32)
                        for half in range(2):
                            moved = pltpu.roll(whole, jnp.bitwise_and(gam * 32 - spot - 32 * half + 256, 127), 2)
                            at = (pl.ds(line * KB + 12 * half, HALF), pl.ds(pl.multiple_of(slot * 32, 32), 32), slice(None))
                            t[at] = jnp.where(inside, moved, t[at].astype(F32)).astype(BF16)
                        return 0

                    lax.fori_loop(0, total, place, 0)

                return slot + jnp.where(hit, 1, 0)

            slot = lax.fori_loop(0, 2, arrival, slot)

        @pl.when(index == 0)
        def _():
            load_w.wait()

        acc[...] = jnp.zeros_like(acc)

        def multiply(block, _):
            def run(source, row, first):
                lhs = [t[block * KB + k] for k in range(KB)]
                rhs = [source[pl.ds(row, 32), first + k].reshape(256, 128) for k in range(KB)]
                acc[...] += lax.dot_general(
                    jnp.concatenate(lhs, axis=1),
                    jnp.concatenate(rhs, axis=1),
                    (((1,), (1,)), ((), ())),
                    preferred_element_type=F32,
                )

            @pl.when(busy[block] == 1)
            def _():
                @pl.when(block >= 2)
                def _():
                    part = w_other.at[pl.ds(alpha * 32, 32), pl.ds((block - 2) * KB, KB)]
                    load = pltpu.make_async_copy(part, spare, spare_sem)
                    load.start()
                    load.wait()
                    run(spare, 0, 0)

                @pl.when(block < 2)
                def _():
                    run(w, alpha * 32, block * KB)

            return 0

        lax.fori_loop(0, 4, multiply, 0)

        def give(j, _):
            value = acc[pl.ds(pl.multiple_of(j * 32, 32), 32), :]

            @pl.when(alpha == core)
            def _():
                keep[blocks[j]] = value

            @pl.when(alpha != core)
            def _():
                send[blocks[j]] = value

            return 0

        lax.fori_loop(0, jnp.minimum(slot, SLOTS), give, 0)
        return 0

    lax.fori_loop(0, 2 * windows, half_of_a, 0)


def last_kernel(lv, lo, tier, parts, other, out):
    gx, gy, gz = lax.axis_index("gx"), lax.axis_index("gy"), lax.axis_index("gz")
    dest = gy * 2 + gz
    shift = lo[4] ^ lo[5]
    for alpha in range(2):
        label = lv[2 * gx + alpha] ^ shift
        cols = []
        for beta in range(2):
            total = jnp.zeros((32, 256), F32)
            for y in range(4):
                for g in range(2):
                    total = total + parts[2 * (y * 4 + alpha * 2 + g) + beta]
            cols.append(jnp.where(lv[2 * dest + beta] == label, total, 0.0))
        rows = slice(alpha * 256, alpha * 256 + 256)
        out[rows, :] = jnp.where(tier[0] == 0, jnp.concatenate(cols, axis=0).T, other[rows, :])


def gather_ring(mine):
    up = [(i, (i // 8) * 8 + (i + 1) % 8) for i in range(16)]
    down = [(i, (i // 8) * 8 + (i + 7) % 8) for i in range(16)]
    cross = [(i, (i + 8) % 16) for i in range(16)]
    zp = lambda v: lax.ppermute(v, "gx", up)
    zm = lambda v: lax.ppermute(v, "gx", down)
    xx = lambda v: lax.ppermute(v, "gx", cross)
    hold = lax.optimization_barrier
    p1, m1, o0 = hold((zp(mine), zm(mine), xx(mine)))
    p2, m2, o1 = hold((zp(p1), zm(m1), xx(m1)))
    p3, m3, o7 = hold((zp(p2), zm(m2), xx(p1)))
    p4, o2, o3 = hold((zp(p3), zm(o1), xx(m3)))
    o6, o4, o5 = hold((zp(o7), zm(o3), xx(p3)))
    return [mine, m1, m2, m3, p4, p3, p2, p1, o0, o1, o2, o3, o4, o5, o6, o7]


def sparse(tier, integrals, amplitude, virtual_irrep, occupied_irrep):
    smem = pl.BlockSpec(memory_space=SMEM)
    vmem = pl.BlockSpec(memory_space=VMEM)
    hbm = pl.BlockSpec(memory_space=pl.ANY)
    chunk = (GROUPS, HALF, 32, 128)
    params = pltpu.CompilerParams(vmem_limit_bytes=32 * 2**20)
    swap = lambda v: lax.ppermute(v, "gy", [(i, i ^ 1) for i in range(8)])
    w = jnp.transpose(integrals, (0, 2, 1, 3))
    amp_other, tier = lax.optimization_barrier((swap(amplitude), tier))
    packed = pl.pallas_call(
        pack_kernel,
        out_shape=jax.ShapeDtypeStruct(chunk, BF16),
        in_specs=[smem, smem, vmem, vmem],
        out_specs=vmem,
        compiler_params=params,
        name="pack",
    )(virtual_irrep, occupied_irrep, amplitude, amp_other)
    packed, w = lax.optimization_barrier((packed, w))
    w_other = swap(w)
    args = integrals, amplitude, virtual_irrep, occupied_irrep
    chunks = gather_ring(packed)
    keep, send = pl.pallas_call(
        main_kernel,
        out_shape=[jax.ShapeDtypeStruct((32, 32, 256), F32)] * 2,
        in_specs=[smem, smem, hbm, hbm] + [vmem] * 16,
        out_specs=[vmem, vmem],
        scratch_shapes=[
            pltpu.VMEM((64, 50, 8, 128), BF16),
            pltpu.VMEM((32, KB, 8, 128), BF16),
            pltpu.VMEM((100, 32 * SLOTS, 128), BF16),
            pltpu.VMEM((32 * SLOTS, 256), F32),
            pltpu.SMEM((32,), I32),
            pltpu.SMEM((2, 8), I32),
            pltpu.SMEM((32,), I32),
            pltpu.SMEM((4,), I32),
            pltpu.SemaphoreType.DMA,
            pltpu.SemaphoreType.DMA,
        ],
        compiler_params=params,
        name="main",
    )(virtual_irrep, occupied_irrep, w, w_other, *chunks)
    parts = lax.all_to_all(keep + swap(send), ("gy", "gz"), 0, 0, tiled=True)
    parts, late = lax.optimization_barrier((parts, tier))
    other = lax.cond(late[0] == 1, lambda: dense(*args), lambda: jnp.zeros((512, 64), F32))
    out = pl.pallas_call(
        last_kernel,
        out_shape=jax.ShapeDtypeStruct((512, 64), F32),
        in_specs=[smem, smem, smem, vmem, vmem],
        out_specs=vmem,
        compiler_params=params,
        name="last",
    )(virtual_irrep, occupied_irrep, tier, parts, other)
    return out.reshape(64, 8, 64)


def dense(integrals, amplitude, virtual_irrep, occupied_irrep):
    rows_a, width_i, rows_k, rows_c = integrals.shape
    vlabels = jnp.repeat(virtual_irrep, VB)
    klabels = jnp.repeat(occupied_irrep[: K // KB], KB)
    irrep_left = occupied_irrep[K // KB]
    irrep_right = occupied_irrep[K // KB + 1]
    a_labels = lax.dynamic_slice_in_dim(vlabels, lax.axis_index("gx") * rows_a, rows_a)
    c_labels = lax.dynamic_slice_in_dim(vlabels, lax.axis_index("gy") * rows_c, rows_c)
    k_labels = lax.dynamic_slice_in_dim(klabels, lax.axis_index("gz") * rows_k, rows_k)
    left_key = a_labels[:, None, None] ^ k_labels[None, :, None] ^ c_labels[None, None, :] ^ irrep_left
    masked = jnp.where((left_key == 0)[:, None, :, :], integrals, jnp.zeros((), integrals.dtype))
    masked = masked.reshape(rows_a * width_i, rows_k, rows_c)
    right_key = k_labels[:, None] ^ c_labels[None, :] ^ irrep_right
    around = gather_ring(amplitude)
    x, z = lax.axis_index("gx") // 8, lax.axis_index("gx") % 8
    piece = jnp.stack([jnp.concatenate(around[:8], axis=1), jnp.concatenate(around[8:], axis=1)])
    piece = jnp.roll(piece.reshape(2, rows_k, 8, 64, rows_c), (x, z), (0, 2))
    piece = piece.transpose(1, 0, 2, 3, 4).reshape(rows_k, 1024, rows_c)
    keep_amp = (right_key[:, None, :] ^ vlabels[None, :, None]) == 0
    terms = lax.dot_general(
        masked,
        jnp.where(keep_amp, piece, jnp.zeros((), piece.dtype)),
        (((1, 2), (0, 2)), ((), ())),
        preferred_element_type=F32,
    )
    terms = terms.reshape(rows_a * width_i, 16, 64).transpose(1, 0, 2)
    share = lax.all_to_all(terms, ("gy", "gz"), 0, 0, tiled=True).sum(0)
    return share


def body(integrals, amplitude, virtual_irrep, occupied_irrep):
    smem = pl.BlockSpec(memory_space=SMEM)
    tier = pl.pallas_call(
        tier_kernel,
        out_shape=jax.ShapeDtypeStruct((1,), I32),
        in_specs=[smem, smem],
        out_specs=smem,
        name="tier",
    )(virtual_irrep, occupied_irrep)
    args = integrals, amplitude, virtual_irrep, occupied_irrep
    return sparse(tier, *args)


def solution(mesh):
    return jax.shard_map(
        body,
        mesh=mesh,
        in_specs=(P("gx", None, "gz", "gy"), P("gz", "gx", "gy"), P(), P()),
        out_specs=P("gx", None, ("gy", "gz")),
        check_vma=False,
    )
```

```python
import functools

import jax
import jax.numpy as jnp
from jax import lax
from jax.experimental import pallas as pl
from jax.experimental.pallas import tpu as pltpu
from jax.sharding import PartitionSpec as P

K = 100
VB = 32
KB = 25
HALF = 13
GROUPS = 3
EARLY = (0, 1, 2, 3, 4, 5, 6, 7, 8, 9, 10, 11, 15)
LATE = (12, 13, 14)
SMEM = pltpu.MemorySpace.SMEM
VMEM = pltpu.MemorySpace.VMEM
I32 = jnp.int32
F32 = jnp.float32
BF16 = jnp.bfloat16


def tier_kernel(lv, lo, out):
    rows = lax.broadcasted_iota(I32, (32, 128), 0)
    lanes = lax.broadcasted_iota(I32, (32, 128), 1)
    col = jnp.zeros((32, 128), I32)
    row = jnp.full((32, 128), 64, I32)
    for block in range(32):
        col = jnp.where(rows == block, lv[block], col)
        row = jnp.where(lanes == block, lv[block], row)
    right = lo[5]
    both = jnp.bitwise_xor(col, row)
    even = (jnp.bitwise_and(rows, 1) == 0) & (lanes < 32)
    load = jnp.zeros((), I32)
    for part in range(2):
        total = jnp.zeros((32, 128), I32)
        for kap in range(2):
            total += jnp.where(both == jnp.bitwise_xor(lo[2 * part + kap], right), 1, 0)
        for shift in (127, 126, 124):
            total = total + pltpu.roll(total, shift, 1)
        total = total + pltpu.roll(total, 31, 0)
        load = jnp.maximum(load, jnp.max(jnp.where(even & (jnp.bitwise_and(lanes, 7) == 0), total, 0)))
    out[0] = jnp.where(load <= 4 * GROUPS, 0, 1)


def pack_kernel(lv, lo, own, other, out):
    gx, gy, gz = lax.axis_index("gx"), lax.axis_index("gy"), lax.axis_index("gz")
    core = gy % 2
    lanes = lax.broadcasted_iota(I32, (HALF, 32, 128), 2)
    rows = lax.broadcasted_iota(I32, (HALF, 32, 128), 0)
    out[...] = jnp.zeros_like(out)
    room = 2 * GROUPS

    def add(amp, plane, mine):
        def step(index, carry):
            seen, unit = carry
            beta, kap, gam = index // 8, (index // 4) % 2, index % 4
            hit = lo[2 * gz + kap] ^ lv[4 * (gy - core + plane) + gam] ^ lv[2 * gx + beta] ^ lo[5] == 0
            put = hit & ((seen < room) == mine) & (unit < room)

            @pl.when(put)
            def _():
                spot = (unit % 2) * 64
                value = out[unit // 2].astype(F32)
                for half in range(2):
                    part = amp[pl.ds(kap * KB + 12 * half, HALF), pl.ds(pl.multiple_of(beta * 32, 32), 32), :]
                    to = spot + 32 * half
                    moved = pltpu.roll(part.astype(F32), jnp.bitwise_and(to - gam * 32 + 128, 127), 2)
                    take = (lanes >= to) & (lanes < to + 32) & (rows >= half)
                    value = jnp.where(take, moved, value)
                out[unit // 2] = value.astype(BF16)

            return seen + jnp.where(hit, 1, 0), unit + jnp.where(put, 1, 0)

        return lambda unit: lax.fori_loop(0, 16, step, (jnp.zeros((), I32), unit))[1]

    unit = add(own, core, True)(jnp.zeros((), I32))
    add(other, 1 - core, False)(unit)


def main_kernel(arrived, slots, lv, lo, w_own, w_other, *refs):
    chunks, refs = dict(zip(arrived, refs)), refs[len(arrived) :]
    before, refs = refs[:-12], refs[-12:]
    keep, send, w, spare, t, acc, pairs, units, blocks, busy, w_sem, spare_sem = refs
    gx, gy, gz = lax.axis_index("gx"), lax.axis_index("gy"), lax.axis_index("gz")
    core = gy % 2
    x, z = gx // 8, gx % 8
    load_w = pltpu.make_async_copy(w_own, w, w_sem)
    load_w.start()
    for i, total in enumerate((keep, send)):
        total[...] = before[i][...] if before else jnp.zeros_like(total)
    room = 2 * GROUPS

    shift = lo[4] ^ lo[5]
    for plane in range(2):
        for label in range(8):
            units[plane, label] = 0
    for plane in range(2):
        first_c = 4 * (gy if plane == 0 else gy + 1 - 2 * core)
        for kap in range(2):
            for gam in range(4):
                label = lo[2 * gz + kap] ^ lv[first_c + gam] ^ lo[5]
                spot = units[plane, label]
                for alpha in range(2):
                    @pl.when(label == lv[2 * gx + alpha] ^ shift)
                    def _():
                        pairs[alpha * 16 + plane * 8 + spot] = kap * 4 + gam
                units[plane, label] = spot + 1
    lanes = lax.broadcasted_iota(I32, (1, 32, 128), 2)

    wants = [lv[2 * gx + alpha] ^ shift for alpha in range(2)]
    most = [jnp.zeros((), I32)] * 2
    for p in arrived:
        source = (x ^ (p // 8)) * 8 + ((z + p) % 8)
        for beta in range(2):
            most = [n + jnp.where(lv[2 * source + beta] == want, 1, 0) for n, want in zip(most, wants)]
    windows = (jnp.maximum(most[0], most[1]) + slots - 1) // slots

    def half_of_a(index, _):
        alpha, window = index // windows, index % windows
        want = lv[2 * gx + alpha] ^ shift
        for block in range(4):
            busy[block] = 0

        slot = -slots * window
        for p in arrived:
            source = (x ^ (p // 8)) * 8 + ((z + p) % 8)

            def arrival(beta, slot, p=p, source=source):
                block = 2 * source + beta
                hit = lv[block] == want

                @pl.when(hit & (slot >= 0) & (slot < slots))
                def _():
                    blocks[slot] = block
                    own_first = jnp.where(beta == 0, 0, units[0, lv[2 * source]])
                    far_first = jnp.where(beta == 0, 0, units[1, lv[2 * source]])
                    own_here = units[0, lv[2 * source]] + units[0, lv[2 * source + 1]]
                    near = jnp.clip(room - own_first, 0, units[0, want])
                    skip = jnp.clip(room - far_first, 0, units[1, want])
                    total = near + units[1, want] - skip

                    def place(i, _):
                        far = jnp.where(i < near, 0, 1)
                        r = jnp.where(far == 0, i, i - near + skip)
                        unit = jnp.minimum(jnp.where(far == 0, own_first + r, own_here + far_first + r - room), room - 1)
                        pair = pairs[alpha * 16 + far * 8 + r]
                        line, gam = far * 2 + pair // 4, pair % 4

                        @pl.when(busy[line] == 0)
                        def _():
                            t[pl.ds(line * KB, KB)] = jnp.zeros((KB, 32 * slots, 128), BF16)
                            busy[line] = 1

                        spot = (unit % 2) * 64
                        whole = chunks[p][unit // 2]
                        inside = ((lanes >= gam * 32) & (lanes < gam * 32 + 32)).astype(F32).astype(BF16)
                        for half in range(2):
                            moved = pltpu.roll(whole, jnp.bitwise_and(gam * 32 - spot - 32 * half + 256, 127), 2)
                            at = (pl.ds(line * KB + 12 * half, HALF), pl.ds(pl.multiple_of(slot * 32, 32), 32), slice(None))
                            t[at] = t[at] + moved * inside
                        return 0

                    lax.fori_loop(0, total, place, 0)

                return slot + jnp.where(hit, 1, 0)

            slot = lax.fori_loop(0, 2, arrival, slot)

        @pl.when(index == 0)
        def _():
            load_w.wait()

        acc[...] = jnp.zeros_like(acc)

        def multiply(block, _):
            def run(source, row, first):
                lhs = [t[block * KB + k] for k in range(KB)]
                rhs = [source[pl.ds(row, 32), first + k].reshape(256, 128) for k in range(KB)]
                acc[...] += lax.dot_general(
                    jnp.concatenate(lhs, axis=1),
                    jnp.concatenate(rhs, axis=1),
                    (((1,), (1,)), ((), ())),
                    preferred_element_type=F32,
                )

            @pl.when(busy[block] == 1)
            def _():
                @pl.when(block >= 2)
                def _():
                    part = w_other.at[pl.ds(alpha * 32, 32), pl.ds((block - 2) * KB, KB)]
                    load = pltpu.make_async_copy(part, spare, spare_sem)
                    load.start()
                    load.wait()
                    run(spare, 0, 0)

                @pl.when(block < 2)
                def _():
                    run(w, alpha * 32, block * KB)

            return 0

        lax.fori_loop(0, 4, multiply, 0)

        def give(j, _):
            value = acc[pl.ds(pl.multiple_of(j * 32, 32), 32), :]

            @pl.when(alpha == core)
            def _():
                keep[blocks[j]] = value

            @pl.when(alpha != core)
            def _():
                send[blocks[j]] = value

            return 0

        lax.fori_loop(0, jnp.minimum(slot, slots), give, 0)
        return 0

    lax.fori_loop(0, 2 * windows, half_of_a, 0)

    @pl.when(windows == 0)
    def _():
        load_w.wait()


def last_kernel(lv, lo, tier, parts, other, out, sem):
    gx, gy, gz = lax.axis_index("gx"), lax.axis_index("gy"), lax.axis_index("gz")
    dest = gy * 2 + gz
    shift = lo[4] ^ lo[5]
    for alpha in range(2):
        label = lv[2 * gx + alpha] ^ shift
        cols = []
        for beta in range(2):
            total = jnp.zeros((32, 256), F32)
            for y in range(4):
                for g in range(2):
                    total = total + parts[2 * (y * 4 + alpha * 2 + g) + beta]
            cols.append(jnp.where(lv[2 * dest + beta] == label, total, 0.0))
        rows = slice(alpha * 256, alpha * 256 + 256)
        out[rows, :] = jnp.concatenate(cols, axis=0).T

    @pl.when(tier[0] == 1)
    def _():
        load = pltpu.make_async_copy(other, out, sem)
        load.start()
        load.wait()


def gather_ring(mine, *extra):
    up = [(i, (i // 8) * 8 + (i + 1) % 8) for i in range(16)]
    down = [(i, (i // 8) * 8 + (i + 7) % 8) for i in range(16)]
    cross = [(i, (i + 8) % 16) for i in range(16)]
    zp = lambda v: lax.ppermute(v, "gx", up)
    zm = lambda v: lax.ppermute(v, "gx", down)
    xx = lambda v: lax.ppermute(v, "gx", cross)
    hold = lax.optimization_barrier
    p1, m1, o0 = hold((zp(mine), zm(mine), xx(mine)))
    p2, m2, o1 = hold((zp(p1), zm(m1), xx(m1)))
    p3, m3, o7, *extra = hold((zp(p2), zm(m2), xx(p1), *extra))
    p4, o2, o3 = hold((zp(p3), zm(o1), xx(m3)))
    o6, o4, o5 = hold((zp(o7), zm(o3), xx(p3)))
    return [mine, m1, m2, m3, p4, p3, p2, p1, o0, o1, o2, o3, o4, o5, o6, o7], *extra


def sparse(tier, integrals, amplitude, virtual_irrep, occupied_irrep):
    smem = pl.BlockSpec(memory_space=SMEM)
    vmem = pl.BlockSpec(memory_space=VMEM)
    hbm = pl.BlockSpec(memory_space=pl.ANY)
    chunk = (GROUPS, HALF, 32, 128)
    params = pltpu.CompilerParams(vmem_limit_bytes=32 * 2**20)
    swap = lambda v: lax.ppermute(v, "gy", [(i, i ^ 1) for i in range(8)])
    w = jnp.transpose(integrals, (0, 2, 1, 3))
    amp_other, tier = lax.optimization_barrier((swap(amplitude), tier))
    packed = pl.pallas_call(
        pack_kernel,
        out_shape=jax.ShapeDtypeStruct(chunk, BF16),
        in_specs=[smem, smem, vmem, vmem],
        out_specs=vmem,
        compiler_params=params,
        name="pack",
    )(virtual_irrep, occupied_irrep, amplitude, amp_other)
    packed, w = lax.optimization_barrier((packed, w))
    args = integrals, amplitude, virtual_irrep, occupied_irrep
    chunks, w_other = gather_ring(packed, swap(w))
    before = []
    for arrived, slots in ((EARLY, 8), (LATE, 4)):
        before = pl.pallas_call(
            functools.partial(main_kernel, arrived, slots),
            out_shape=[jax.ShapeDtypeStruct((32, 32, 256), F32)] * 2,
            in_specs=[smem, smem, hbm, hbm] + [vmem] * (len(arrived) + len(before)),
            out_specs=[vmem, vmem],
            scratch_shapes=[
                pltpu.VMEM((64, 50, 8, 128), BF16),
                pltpu.VMEM((32, KB, 8, 128), BF16),
                pltpu.VMEM((100, 32 * slots, 128), BF16),
                pltpu.VMEM((32 * slots, 256), F32),
                pltpu.SMEM((32,), I32),
                pltpu.SMEM((2, 8), I32),
                pltpu.SMEM((32,), I32),
                pltpu.SMEM((4,), I32),
                pltpu.SemaphoreType.DMA,
                pltpu.SemaphoreType.DMA,
            ],
            compiler_params=params,
            cost_estimate=pl.CostEstimate(flops=slots * 10**9, bytes_accessed=slots * 3 * 10**6, transcendentals=0),
            name="main" if slots == 8 else "rest",
        )(virtual_irrep, occupied_irrep, w, w_other, *[chunks[p] for p in arrived], *before)
    keep, send = before
    parts = lax.all_to_all(keep + swap(send), ("gy", "gz"), 0, 0, tiled=True)
    parts, late = lax.optimization_barrier((parts, tier))
    other = lax.cond(late[0] == 1, lambda: dense(*args), lambda: jnp.zeros((512, 64), F32))
    out = pl.pallas_call(
        last_kernel,
        out_shape=jax.ShapeDtypeStruct((512, 64), F32),
        in_specs=[smem, smem, smem, vmem, hbm],
        out_specs=vmem,
        scratch_shapes=[pltpu.SemaphoreType.DMA],
        compiler_params=params,
        name="last",
    )(virtual_irrep, occupied_irrep, tier, parts, other)
    return out.reshape(64, 8, 64)


def dense(integrals, amplitude, virtual_irrep, occupied_irrep):
    rows_a, width_i, rows_k, rows_c = integrals.shape
    vlabels = jnp.repeat(virtual_irrep, VB)
    klabels = jnp.repeat(occupied_irrep[: K // KB], KB)
    irrep_left = occupied_irrep[K // KB]
    irrep_right = occupied_irrep[K // KB + 1]
    a_labels = lax.dynamic_slice_in_dim(vlabels, lax.axis_index("gx") * rows_a, rows_a)
    c_labels = lax.dynamic_slice_in_dim(vlabels, lax.axis_index("gy") * rows_c, rows_c)
    k_labels = lax.dynamic_slice_in_dim(klabels, lax.axis_index("gz") * rows_k, rows_k)
    left_key = a_labels[:, None, None] ^ k_labels[None, :, None] ^ c_labels[None, None, :] ^ irrep_left
    masked = jnp.where((left_key == 0)[:, None, :, :], integrals, jnp.zeros((), integrals.dtype))
    masked = masked.reshape(rows_a * width_i, rows_k, rows_c)
    right_key = k_labels[:, None] ^ c_labels[None, :] ^ irrep_right
    around, = gather_ring(amplitude)
    x, z = lax.axis_index("gx") // 8, lax.axis_index("gx") % 8
    piece = jnp.stack([jnp.concatenate(around[:8], axis=1), jnp.concatenate(around[8:], axis=1)])
    piece = jnp.roll(piece.reshape(2, rows_k, 8, 64, rows_c), (x, z), (0, 2))
    piece = piece.transpose(1, 0, 2, 3, 4).reshape(rows_k, 1024, rows_c)
    keep_amp = (right_key[:, None, :] ^ vlabels[None, :, None]) == 0
    terms = lax.dot_general(
        masked,
        jnp.where(keep_amp, piece, jnp.zeros((), piece.dtype)),
        (((1, 2), (0, 2)), ((), ())),
        preferred_element_type=F32,
    )
    terms = terms.reshape(rows_a * width_i, 16, 64).transpose(1, 0, 2)
    share = lax.all_to_all(terms, ("gy", "gz"), 0, 0, tiled=True).sum(0)
    return share


def body(integrals, amplitude, virtual_irrep, occupied_irrep):
    smem = pl.BlockSpec(memory_space=SMEM)
    tier = pl.pallas_call(
        tier_kernel,
        out_shape=jax.ShapeDtypeStruct((1,), I32),
        in_specs=[smem, smem],
        out_specs=smem,
        name="tier",
    )(virtual_irrep, occupied_irrep)
    args = integrals, amplitude, virtual_irrep, occupied_irrep
    return sparse(tier, *args)


def solution(mesh):
    return jax.shard_map(
        body,
        mesh=mesh,
        in_specs=(P("gx", None, "gz", "gy"), P("gz", "gx", "gy"), P(), P()),
        out_specs=P("gx", None, ("gy", "gz")),
        check_vma=False,
    )
```
